512 devices in a mesh: dp: 32 (over x_lo, z), tensor: 16 (over y, x_hi, core).
Axes of the slice: x: 4 (x_hi: 2, x_lo: 2; x = x_hi * 2 + x_lo), y: 4, z: 16, core: 2. Of those that a mesh axis runs over, the one named last changes fastest.
Arguments:
- gate_pre: bfloat16 [2048, 6656], P('dp', 'tensor'), may hold values from -6 to 6
- up_pre: bfloat16 [2048, 6656], P('dp', 'tensor'), may hold values from -6 to 6
- out_grad: bfloat16 [2048, 16384], P('tensor', 'dp'), may hold values from -6 to 6
- down_weight: bfloat16 [6656, 16384], P('tensor', 'dp'), may hold values from -0.046875 to 0.046875
Outputs:
- gate_grad: bfloat16 [2048, 6656], P('dp', 'tensor')
- up_grad: bfloat16 [2048, 6656], P('dp', 'tensor')
- weight_grad: float32 [6656, 16384], P('tensor', 'dp')
The draws below stay inside these ranges and needn't reach their ends.
All inputs are finite; a program needn't handle non-finite values.
Results may differ from the reference program's by a relative error of at most 0.0029.
Values may be sent and summed in bfloat16 or wider, within the bound.
No kernel may reach another device: no remote copies, remote signals or barrier semaphores. Data moves between devices by JAX's collectives and lax.ppermute only.
A program may use at most 64 MiB of HBM per device.

```python
import jax
import jax.numpy as jnp
from jax import lax

D = 16384
FF = 6656
TOKENS = 2048


def with_spikes(result, rng, source, target, parts, factor):
    owner, partner = [(jnp.arange(result.shape[position]) // (result.shape[position] // parts)).reshape([-1 if axis == position else 1 for axis in range(result.ndim)]) for position in (source, target)]
    chosen = jax.random.permutation(rng, parts)[partner]
    strong = (owner == chosen) | (owner == (partner + parts // 2) % parts)
    return jnp.where(strong, factor * result, result)


def levels(stream_key, dims, split, least, high):
    gain, own = 1.0, jax.random.fold_in(stream_key, 6)
    for dim, parts in split:
        heights = jnp.exp(jax.random.uniform(jax.random.fold_in(own, dim), (parts,), jnp.float32, least / len(split), high / len(split)))
        gain = gain * jnp.repeat(heights, dims[dim] // parts).reshape([-1 if axis == dim else 1 for axis in range(len(dims))])
    return gain


def noise(key, dims, spread, reach, shards=(), dtype=jnp.bfloat16):
    values = spread * jax.random.normal(key, dims, jnp.float32)
    if shards:
        values = values * levels(key, dims, shards, -0.22, 0.18)
    return jnp.clip(values, -reach, reach).astype(dtype)


def heavy_noise(own_key, shape, spread, reach, shards, heavy, dtype=jnp.bfloat16):
    drawn = spread * jax.random.normal(own_key, shape, jnp.float32)
    if shards:
        drawn = drawn * levels(own_key, shape, shards, -0.22, 0.18)
    return jnp.clip(with_spikes(drawn, jax.random.fold_in(own_key, 3), *heavy), -reach, reach).astype(dtype)


def setup_inputs(seed: int = 0) -> dict:
    splits = jax.random.split(jax.random.key(seed), 5)
    gate_pre = noise(splits[0], (TOKENS, FF), 1.0, 6.0, ((0, 32), (1, 16)))
    up_pre = noise(splits[1], (TOKENS, FF), 1.0, 6.0, ((0, 32), (1, 16)))
    out_grad = heavy_noise(splits[2], (TOKENS, D), 1.0, 6.0, ((0, 16), (1, 32)), (1, 0, 32, 2.75))
    down_weight = noise(splits[3], (FF, D), D ** -0.5, 0.046875, ((0, 16), (1, 32)))
    return {"gate_pre": gate_pre, "up_pre": up_pre, "out_grad": out_grad, "down_weight": down_weight}


def reference(gate_pre, up_pre, out_grad, down_weight):
    gate_vals = gate_pre.astype(jnp.float32)
    up_vals = up_pre.astype(jnp.float32)
    sigmoid_gate = jax.nn.sigmoid(gate_vals)
    activated = gate_vals * sigmoid_gate
    hidden = (activated * up_vals).astype(jnp.bfloat16)
    hidden_grad = lax.dot_general(out_grad, down_weight, (((1,), (1,)), ((), ())), preferred_element_type=jnp.float32)
    gate_grad = (hidden_grad * up_vals * sigmoid_gate * (1.0 + gate_vals * (1.0 - sigmoid_gate))).astype(jnp.bfloat16)
    up_grad = (hidden_grad * activated).astype(jnp.bfloat16)
    weight_grad = jnp.dot(hidden.T, out_grad, preferred_element_type=jnp.float32) * (TOKENS ** -0.5)
    return gate_grad, up_grad, weight_grad
```

```python
import jax
import jax.numpy as jnp
import numpy as np
from jax import lax
from jax.sharding import Mesh, PartitionSpec as P

Z = ("z3", "z2", "z1", "z0")
DP = ("xl",) + Z
YX = ("y1", "y0", "xh")
TENSOR = YX + ("c",)
SWAP = [(0, 1), (1, 0)]


def to_half(rows):
    top = jnp.max(jnp.abs(rows), axis=-1, keepdims=True)
    exponent = jnp.floor(jnp.log2(jnp.maximum(top, 1e-37)))
    scaled = (rows * jnp.exp2(-exponent)).astype(jnp.float16)
    return jnp.concatenate([scaled, exponent.astype(jnp.float16)], axis=-1)


def from_half(coded):
    return coded[..., :-1].astype(jnp.float32) * jnp.exp2(coded[..., -1:].astype(jnp.float32))


def times(grad, weight):
    return lax.dot_general(
        grad, weight, (((grad.ndim - 1,), (1,)), ((), ())), preferred_element_type=jnp.float32
    )


def shards(gate_pre, up_pre, out_grad, down_weight):
    xl, c = lax.axis_index("xl"), lax.axis_index("c")
    rows, hid = gate_pre.shape
    feats = out_grad.shape[1]
    gate_vals = gate_pre.astype(jnp.float32)
    sigmoid_gate = jax.nn.sigmoid(gate_vals)
    activated = gate_vals * sigmoid_gate
    up_vals = up_pre.astype(jnp.float32)
    hidden = (activated * up_vals).astype(jnp.bfloat16)

    theirs = lax.ppermute(hidden, "xl", SWAP)
    pair = jnp.where(xl == 0, jnp.stack([hidden, theirs]), jnp.stack([theirs, hidden]))
    hidden_all = lax.all_gather(pair, Z, axis=0)

    mine = lax.all_to_all(jnp.broadcast_to(out_grad[None], (8,) + out_grad.shape), YX, 0, 0)
    other = lax.ppermute(mine, "c", SWAP)
    grad_all = jnp.where(c == 0, jnp.stack([mine, other], 1), jnp.stack([other, mine], 1))
    halves = grad_all.reshape(2, 16 * rows, feats)

    sent = times(lax.dynamic_index_in_dim(halves, 1 - xl, 0, False), down_weight)
    got = lax.ppermute(to_half(sent), "xl", SWAP)
    kept = times(lax.dynamic_index_in_dim(halves, xl, 0, False), down_weight)
    summed = to_half(kept + from_half(got)).reshape(16, rows, hid + 1)
    hidden_grad = jnp.sum(from_half(lax.all_to_all(summed, Z, 0, 0)), axis=0)

    gate_grad = (
        hidden_grad * up_vals * sigmoid_gate * (1.0 + gate_vals * (1.0 - sigmoid_gate))
    ).astype(jnp.bfloat16)
    up_grad = (hidden_grad * activated).astype(jnp.bfloat16)

    tokens = hidden_all.transpose(1, 0, 2, 3).reshape(32 * rows, hid)
    weight_grad = lax.dot_general(
        tokens, grad_all.reshape(32 * rows, feats), (((0,), (0,)), ((), ())), preferred_element_type=jnp.float32
    ) * (32 * rows) ** (-0.5)
    return (gate_grad, up_grad, weight_grad)


def solution(mesh):
    bits = Mesh(np.asarray(mesh.devices).reshape((2,) * 9), DP + TENSOR)
    return jax.shard_map(
        shards,
        mesh=bits,
        in_specs=(P(DP, TENSOR), P(DP, TENSOR), P(TENSOR, DP), P(TENSOR, DP)),
        out_specs=(P(DP, TENSOR), P(DP, TENSOR), P(TENSOR, DP)),
        check_vma=False,
    )
```

```python
import functools

import jax
import jax.numpy as jnp
import numpy as np
from jax import lax
from jax.experimental import pallas as pl
from jax.experimental.pallas import tpu as pltpu
from jax.sharding import Mesh, PartitionSpec as P

Z = ("z3", "z2", "z1", "z0")
FAR = Z[:2]
DP = ("xl",) + Z
YX = ("y1", "y0", "xh")
TENSOR = YX + ("c",)
SWAP = [(0, 1), (1, 0)]
LANES = 128
VMEM_BYTES = 32 * 1024 * 1024
whole = pl.BlockSpec(memory_space=pltpu.VMEM)
scalars = pl.BlockSpec(memory_space=pltpu.SMEM)


def pack(block):
    tail = block[:, 3 * LANES :]
    packed = tail[0:16]
    for k in range(1, 4):
        packed += pltpu.roll(tail[16 * k : 16 * k + 16], 32 * k, 1)
    return jnp.concatenate([block[:, LANES * k : LANES * (k + 1)] for k in range(3)] + [packed], axis=0)


def encode(packed):
    top = jnp.max(jnp.max(jnp.abs(packed), axis=0, keepdims=True), axis=1, keepdims=True)
    exponent = jnp.floor(jnp.log2(jnp.maximum(top, 1e-37)))
    scaled = packed * jnp.exp2(-exponent)
    return jnp.concatenate([scaled, jnp.broadcast_to(exponent, (16, LANES))], axis=0)


def decode(coded):
    return coded[:208] * jnp.exp2(coded[208:209])


def times(rows, weight):
    return lax.dot_general(rows, weight, (((1,), (1,)), ((), ())), preferred_element_type=jnp.float32)


def send_kernel(place_ref, rows_ref, weight_ref, out_ref, padded):
    hid = weight_ref.shape[0]
    padded[hid:] = jnp.zeros_like(padded[hid:])
    padded[:hid] = weight_ref[...]
    rows = rows_ref[pl.ds((1 - place_ref[0]) * 4, 4)].reshape(512, rows_ref.shape[2])
    product = times(rows, padded[...])
    for far in range(4):
        for half in range(2):
            start = far * 128 + half * 64
            out_ref[half, far] = encode(pack(product[start : start + 64]))


def send_part(place, rows, weight):
    return pl.pallas_call(
        send_kernel,
        out_shape=jax.ShapeDtypeStruct((2, 4, 224, LANES), jnp.float32),
        in_specs=[scalars] + [whole] * 2,
        out_specs=whole,
        scratch_shapes=[pltpu.VMEM((512, weight.shape[1]), weight.dtype)],
        compiler_params=pltpu.CompilerParams(vmem_limit_bytes=VMEM_BYTES),
        cost_estimate=pl.CostEstimate(flops=2 * 512 * 512 * 512, bytes_accessed=2 << 20, transcendentals=0),
        name="send_part",
    )(place, rows, weight)


def keep_kernel(place_ref, mine_ref, other_ref, weight_ref, got_mine_ref, got_other_ref, out_ref, padded):
    hid = weight_ref.shape[0]
    padded[hid:] = jnp.zeros_like(padded[hid:])
    padded[:hid] = weight_ref[...]
    xl, c = place_ref[0], place_ref[1]
    for ref, got_ref, core in ((mine_ref, got_mine_ref, c), (other_ref, got_other_ref, 1 - c)):
        rows = ref[pl.ds(xl * 4, 4)].reshape(512, ref.shape[2])
        product = times(rows, padded[...])
        for far in range(4):
            for half in range(2):
                start = far * 128 + half * 64
                vals = pack(product[start : start + 64]) + decode(got_ref[half, far])
                out_ref[core, half, far] = encode(vals)


def keep_part(place, mine, other, weight, got_mine, got_other):
    return pl.pallas_call(
        keep_kernel,
        out_shape=jax.ShapeDtypeStruct((2, 2, 4, 224, LANES), jnp.float32),
        in_specs=[scalars] + [whole] * 5,
        out_specs=whole,
        scratch_shapes=[pltpu.VMEM((512, weight.shape[1]), weight.dtype)],
        compiler_params=pltpu.CompilerParams(vmem_limit_bytes=VMEM_BYTES),
        cost_estimate=pl.CostEstimate(flops=2 * 1024 * 512 * 512, bytes_accessed=4 << 20, transcendentals=0),
        name="keep_part",
    )(place, mine, other, weight, got_mine, got_other)


def merge_kernel(place_ref, got_ref, own_ref, *out_refs):
    for k in range(4):
        far = lax.rem(place_ref[2] + k, 4)
        vals = decode(got_ref[0, far])
        for near in range(1, 4):
            vals += decode(got_ref[near, far])
        if k == 0:
            own_ref[...] = vals
        else:
            out_refs[k - 1][...] = encode(vals)


def merge(place, got):
    return pl.pallas_call(
        merge_kernel,
        out_shape=(jax.ShapeDtypeStruct((208, LANES), jnp.float32),)
        + (jax.ShapeDtypeStruct((224, LANES), jnp.float32),) * 3,
        in_specs=[scalars, whole],
        out_specs=(whole,) * 4,
        compiler_params=pltpu.CompilerParams(vmem_limit_bytes=VMEM_BYTES),
        cost_estimate=pl.CostEstimate(flops=1 << 20, bytes_accessed=1 << 20, transcendentals=0),
        name="merge_parts",
    )(place, got)


def final_kernel(own_ref, a_ref, b_ref, d_ref, gate_ref, up_ref, gate_grad_ref, up_grad_ref):
    packed = own_ref[...] + decode(a_ref[...]) + decode(b_ref[...]) + decode(d_ref[...])
    tail = packed[192:208]
    tails = jnp.concatenate([tail] + [pltpu.roll(tail, LANES - 32 * k, 1) for k in range(1, 4)], axis=0)
    width = gate_ref.shape[1]
    for k in range(4):
        cols = slice(LANES * k, min(LANES * (k + 1), width))
        grad = packed[64 * k : 64 * k + 64] if k < 3 else tails[:, : width - 3 * LANES]
        gate = gate_ref[:, cols].astype(jnp.float32)
        up = up_ref[:, cols].astype(jnp.float32)
        s = jax.nn.sigmoid(gate)
        gate_grad_ref[:, cols] = (grad * up * s * (1.0 + gate * (1.0 - s))).astype(gate_grad_ref.dtype)
        up_grad_ref[:, cols] = (grad * (gate * s)).astype(up_grad_ref.dtype)


def final(parts, gate_pre, up_pre):
    return pl.pallas_call(
        final_kernel,
        out_shape=(jax.ShapeDtypeStruct(gate_pre.shape, gate_pre.dtype),) * 2,
        in_specs=[whole] * 6,
        out_specs=(whole, whole),
        compiler_params=pltpu.CompilerParams(vmem_limit_bytes=VMEM_BYTES),
        cost_estimate=pl.CostEstimate(flops=1, bytes_accessed=1, transcendentals=0),
        name="finish_grads",
    )(*parts, gate_pre, up_pre)


def weight_kernel(place_ref, near_ref, up1_ref, down1_ref, up2_ref, down2_ref, mine_ref, other_ref, out_ref, tokens):
    c, z = place_ref[1], place_ref[3]
    for ref, shift, begin, count in (
        (near_ref, 0, 0, 4),
        (up1_ref, -1, 0, 4),
        (down1_ref, 1, 0, 4),
        (up2_ref, -2, 1, 2),
        (down2_ref, 2, 0, 2),
    ):
        for k in range(count):
            owner = lax.rem(z + shift - 4 * (begin + k - 1) + 32, 16)
            core = lax.rem(owner // 2, 2)
            for xl in range(2):
                start = pl.multiple_of(lax.rem(owner, 2) * 64, 64)
                tokens[xl, core, owner // 4, pl.ds(start, 64)] = ref[k, xl]
    hid = out_ref.shape[0]
    total = None
    for xl in range(2):
        for ref, core in ((mine_ref, c), (other_ref, 1 - c)):
            rows = ref[4 * xl : 4 * xl + 4].reshape(512, ref.shape[2])
            hidden = tokens[xl, core].reshape(512, tokens.shape[4])
            product = lax.dot_general(hidden, rows, (((0,), (0,)), ((), ())), preferred_element_type=jnp.float32)
            total = product if total is None else total + product
    out_ref[...] = total[:hid] * 2048 ** (-0.5)


def weight_part(place, blocks, mine, other, hid):
    return pl.pallas_call(
        weight_kernel,
        out_shape=jax.ShapeDtypeStruct((hid, mine.shape[2]), jnp.float32),
        in_specs=[scalars] + [whole] * 7,
        out_specs=whole,
        scratch_shapes=[pltpu.VMEM((2, 2, 4, 128, 512), mine.dtype)],
        compiler_params=pltpu.CompilerParams(vmem_limit_bytes=VMEM_BYTES),
        cost_estimate=pl.CostEstimate(flops=2 * 2048 * 512 * 512, bytes_accessed=5 << 20, transcendentals=0),
        name="weight_grad",
    )(place, *blocks, mine, other)


def shift(array, axes, step):
    size = 2 ** len(axes)
    return lax.ppermute(array, axes, [(i, (i + step) % size) for i in range(size)])


def shards(gate_pre, up_pre, out_grad, down_weight):
    xl = lax.axis_index("xl")
    place = jnp.stack([xl, lax.axis_index("c"), lax.axis_index(FAR), lax.axis_index(Z)]).astype(jnp.int32)
    hid = gate_pre.shape[1]
    gate_vals = gate_pre.astype(jnp.float32)
    hidden = (gate_vals * jax.nn.sigmoid(gate_vals) * up_pre.astype(jnp.float32)).astype(jnp.bfloat16)
    hidden = jnp.pad(hidden, ((0, 0), (0, 512 - hid)))

    theirs = lax.ppermute(hidden, "xl", SWAP)
    pair = jnp.where(xl == 0, jnp.stack([hidden, theirs]), jnp.stack([theirs, hidden]))
    steps = [shift(pair, FAR, k) for k in (3, 1, 2)]

    mine = lax.all_to_all(jnp.broadcast_to(out_grad[None], (8,) + out_grad.shape), YX, 0, 0)
    other = lax.ppermute(mine, "c", SWAP)

    sent = [send_part(place, rows, down_weight).astype(jnp.float16) for rows in (mine, other)]
    sent, pair, steps = lax.optimization_barrier((sent, pair, steps))
    got = [lax.ppermute(s, "xl", SWAP) for s in sent]

    near = jnp.stack([steps[0], pair, steps[1], steps[2]])
    blocks = [near, shift(near, Z, 1), shift(near, Z, -1), shift(near[1:3], Z, 2), shift(near[0:2], Z, -2)]
    got, blocks = lax.optimization_barrier((got, blocks))

    kept = keep_part(place, mine, other, down_weight, *[g.astype(jnp.float32) for g in got])
    kept = kept.astype(jnp.float16).reshape(4, 4, 224, LANES)
    merged = merge(place, lax.all_to_all(kept, ("z1", "z0"), 0, 0).astype(jnp.float32))
    far = [shift(merged[k].astype(jnp.float16), FAR, k).astype(jnp.float32) for k in range(1, 4)]
    gate_grad, up_grad = final([merged[0]] + far, gate_pre, up_pre)

    weight_grad = weight_part(place, blocks, mine, other, hid)
    return (gate_grad, up_grad, weight_grad)


def solution(mesh):
    bits = Mesh(np.asarray(mesh.devices).reshape((2,) * 9), DP + TENSOR)
    return jax.shard_map(
        shards,
        mesh=bits,
        in_specs=(P(DP, TENSOR), P(DP, TENSOR), P(TENSOR, DP), P(TENSOR, DP)),
        out_specs=(P(DP, TENSOR), P(DP, TENSOR), P(TENSOR, DP)),
        check_vma=False,
    )
```

```python
import functools

import jax
import jax.numpy as jnp
import numpy as np
from jax import lax
from jax.experimental import pallas as pl
from jax.experimental.pallas import tpu as pltpu
from jax.sharding import Mesh, PartitionSpec as P

Z = ("z3", "z2", "z1", "z0")
FAR = Z[:2]
DP = ("xl",) + Z
YX = ("y1", "y0", "xh")
TENSOR = YX + ("c",)
SWAP = [(0, 1), (1, 0)]
LANES = 128
VMEM_BYTES = 32 * 1024 * 1024
whole = pl.BlockSpec(memory_space=pltpu.VMEM)
scalars = pl.BlockSpec(memory_space=pltpu.SMEM)


def pack(block):
    tail = block[:, 3 * LANES :]
    packed = tail[0:16]
    for k in range(1, 4):
        packed += pltpu.roll(tail[16 * k : 16 * k + 16], 32 * k, 1)
    return jnp.concatenate([block[:, LANES * k : LANES * (k + 1)] for k in range(3)] + [packed], axis=0)


def encode(packed):
    top = jnp.max(jnp.max(jnp.abs(packed), axis=0, keepdims=True), axis=1, keepdims=True)
    exponent = jnp.floor(jnp.log2(jnp.maximum(top, 1e-37)))
    scaled = packed * jnp.exp2(-exponent)
    return jnp.concatenate([scaled, jnp.broadcast_to(exponent, (16, LANES))], axis=0)


def decode(coded):
    return coded[:208] * jnp.exp2(coded[208:209])


def times(rows, weight):
    return lax.dot_general(rows, weight, (((1,), (1,)), ((), ())), preferred_element_type=jnp.float32)


def send_kernel(place_ref, rows_ref, weight_ref, out_ref, padded):
    hid = weight_ref.shape[0]
    padded[hid:] = jnp.zeros_like(padded[hid:])
    padded[:hid] = weight_ref[...]
    rows = rows_ref[pl.ds((1 - place_ref[0]) * 4, 4)].reshape(512, rows_ref.shape[2])
    product = times(rows, padded[...])
    for far in range(4):
        for half in range(2):
            start = far * 128 + half * 64
            out_ref[half, far] = encode(pack(product[start : start + 64]))


def send_part(place, rows, weight):
    return pl.pallas_call(
        send_kernel,
        out_shape=jax.ShapeDtypeStruct((2, 4, 224, LANES), jnp.float32),
        in_specs=[scalars] + [whole] * 2,
        out_specs=whole,
        scratch_shapes=[pltpu.VMEM((512, weight.shape[1]), weight.dtype)],
        compiler_params=pltpu.CompilerParams(vmem_limit_bytes=VMEM_BYTES),
        cost_estimate=pl.CostEstimate(flops=2 * 512 * 512 * 512, bytes_accessed=2 << 20, transcendentals=0),
        name="send_part",
    )(place, rows, weight)


def keep_kernel(place_ref, mine_ref, other_ref, weight_ref, got_mine_ref, got_other_ref, out_ref, padded):
    hid = weight_ref.shape[0]
    padded[hid:] = jnp.zeros_like(padded[hid:])
    padded[:hid] = weight_ref[...]
    xl, c = place_ref[0], place_ref[1]
    for ref, got_ref, core in ((mine_ref, got_mine_ref, c), (other_ref, got_other_ref, 1 - c)):
        rows = ref[pl.ds(xl * 4, 4)].reshape(512, ref.shape[2])
        product = times(rows, padded[...])
        for far in range(4):
            for half in range(2):
                start = far * 128 + half * 64
                vals = pack(product[start : start + 64]) + decode(got_ref[half, far])
                out_ref[core, half, far] = encode(vals)


def keep_part(place, mine, other, weight, got_mine, got_other):
    return pl.pallas_call(
        keep_kernel,
        out_shape=jax.ShapeDtypeStruct((2, 2, 4, 224, LANES), jnp.float32),
        in_specs=[scalars] + [whole] * 5,
        out_specs=whole,
        scratch_shapes=[pltpu.VMEM((512, weight.shape[1]), weight.dtype)],
        compiler_params=pltpu.CompilerParams(vmem_limit_bytes=VMEM_BYTES),
        cost_estimate=pl.CostEstimate(flops=2 * 1024 * 512 * 512, bytes_accessed=4 << 20, transcendentals=0),
        name="keep_part",
    )(place, mine, other, weight, got_mine, got_other)


def merge_kernel(place_ref, got_ref, own_ref, *out_refs):
    for k in range(4):
        far = lax.rem(place_ref[2] + k, 4)
        vals = decode(got_ref[0, far])
        for near in range(1, 4):
            vals += decode(got_ref[near, far])
        if k == 0:
            own_ref[...] = vals
        else:
            out_refs[k - 1][...] = encode(vals)


def merge(place, got):
    return pl.pallas_call(
        merge_kernel,
        out_shape=(jax.ShapeDtypeStruct((208, LANES), jnp.float32),)
        + (jax.ShapeDtypeStruct((224, LANES), jnp.float32),) * 3,
        in_specs=[scalars, whole],
        out_specs=(whole,) * 4,
        compiler_params=pltpu.CompilerParams(vmem_limit_bytes=VMEM_BYTES),
        cost_estimate=pl.CostEstimate(flops=1 << 20, bytes_accessed=1 << 20, transcendentals=0),
        name="merge_parts",
    )(place, got)


def final_kernel(own_ref, a_ref, b_ref, d_ref, gate_ref, up_ref, gate_grad_ref, up_grad_ref):
    packed = own_ref[...] + decode(a_ref[...]) + decode(b_ref[...]) + decode(d_ref[...])
    tail = packed[192:208]
    tails = jnp.concatenate([tail] + [pltpu.roll(tail, LANES - 32 * k, 1) for k in range(1, 4)], axis=0)
    width = gate_ref.shape[1]
    for k in range(4):
        cols = slice(LANES * k, min(LANES * (k + 1), width))
        grad = packed[64 * k : 64 * k + 64] if k < 3 else tails[:, : width - 3 * LANES]
        gate = gate_ref[:, cols].astype(jnp.float32)
        up = up_ref[:, cols].astype(jnp.float32)
        s = jax.nn.sigmoid(gate)
        gate_grad_ref[:, cols] = (grad * up * s * (1.0 + gate * (1.0 - s))).astype(gate_grad_ref.dtype)
        up_grad_ref[:, cols] = (grad * (gate * s)).astype(up_grad_ref.dtype)


def final(parts, gate_pre, up_pre):
    return pl.pallas_call(
        final_kernel,
        out_shape=(jax.ShapeDtypeStruct(gate_pre.shape, gate_pre.dtype),) * 2,
        in_specs=[whole] * 6,
        out_specs=(whole, whole),
        compiler_params=pltpu.CompilerParams(vmem_limit_bytes=VMEM_BYTES),
        cost_estimate=pl.CostEstimate(flops=1, bytes_accessed=1, transcendentals=0),
        name="finish_grads",
    )(*parts, gate_pre, up_pre)


def collect_kernel(place_ref, near_ref, up1_ref, down1_ref, up2_ref, down2_ref, out_ref):
    z = place_ref[3]
    for ref, step, begin, count in (
        (near_ref, 0, 0, 4),
        (up1_ref, -1, 0, 4),
        (down1_ref, 1, 0, 4),
        (up2_ref, -2, 1, 2),
        (down2_ref, 2, 0, 2),
    ):
        for k in range(count):
            owner = lax.rem(z + step - 4 * (begin + k - 1) + 32, 16)
            start = pl.multiple_of(lax.rem(owner, 2) * 64, 64)
            out_ref[lax.rem(owner // 2, 2), owner // 4, pl.ds(start, 64)] = ref[k]


def collect(place, blocks):
    near = blocks[0]
    return pl.pallas_call(
        collect_kernel,
        out_shape=jax.ShapeDtypeStruct((2, 4, 128, near.shape[2]), near.dtype),
        in_specs=[scalars] + [whole] * 5,
        out_specs=whole,
        compiler_params=pltpu.CompilerParams(vmem_limit_bytes=VMEM_BYTES),
        cost_estimate=pl.CostEstimate(flops=1 << 20, bytes_accessed=2 << 20, transcendentals=0),
        name="collect_hidden",
    )(place, *blocks)


def weight_kernel(last, place_ref, hidden_ref, mine_ref, other_ref, *refs):
    before_ref, out_ref = refs if last else (None, refs[0])
    xl, c = place_ref[0], place_ref[1]
    first = ((1 - xl) if last else xl) * 4
    hid = out_ref.shape[0]
    total = None
    for ref, core in ((mine_ref, c), (other_ref, 1 - c)):
        rows = ref[pl.ds(first, 4)].reshape(512, ref.shape[2])
        tokens = hidden_ref[core].reshape(512, hidden_ref.shape[3])
        product = lax.dot_general(tokens, rows, (((0,), (0,)), ((), ())), preferred_element_type=jnp.float32)
        total = product if total is None else total + product
    total = total[:hid]
    out_ref[...] = (before_ref[...] + total) * 2048 ** (-0.5) if last else total


def weight_part(place, hidden, mine, other, hid, before=None):
    last = before is not None
    return pl.pallas_call(
        functools.partial(weight_kernel, last),
        out_shape=jax.ShapeDtypeStruct((hid, mine.shape[2]), jnp.float32),
        in_specs=[scalars] + [whole] * (4 if last else 3),
        out_specs=whole,
        compiler_params=pltpu.CompilerParams(vmem_limit_bytes=VMEM_BYTES),
        cost_estimate=pl.CostEstimate(flops=2 * 1024 * 512 * 512, bytes_accessed=4 << 20, transcendentals=0),
        name="weight_part",
    )(place, hidden, mine, other, *([before] if last else []))


def shift(array, axes, step):
    size = 2 ** len(axes)
    return lax.ppermute(array, axes, [(i, (i + step) % size) for i in range(size)])


def shards(gate_pre, up_pre, out_grad, down_weight):
    place = jnp.stack([lax.axis_index("xl"), lax.axis_index("c"), lax.axis_index(FAR), lax.axis_index(Z)]).astype(jnp.int32)
    hid = gate_pre.shape[1]
    gate_vals = gate_pre.astype(jnp.float32)
    hidden = (gate_vals * jax.nn.sigmoid(gate_vals) * up_pre.astype(jnp.float32)).astype(jnp.bfloat16)
    hidden = jnp.pad(hidden, ((0, 0), (0, 512 - hid)))

    mine = lax.all_to_all(jnp.broadcast_to(out_grad[None], (8,) + out_grad.shape), YX, 0, 0)
    steps = [shift(hidden, FAR, k) for k in (3, 1, 2)]
    mine, hidden, steps = lax.optimization_barrier((mine, hidden, steps))
    other = lax.ppermute(mine, "c", SWAP)

    sent = [send_part(place, rows, down_weight).astype(jnp.float16) for rows in (mine, other)]
    near = jnp.stack([steps[0], hidden, steps[1], steps[2]])
    sent, near = lax.optimization_barrier((sent, near))
    got = [lax.ppermute(s, "xl", SWAP) for s in sent]
    blocks = [near, shift(near, Z, 1), shift(near, Z, -1), shift(near[1:3], Z, 2), shift(near[0:2], Z, -2)]
    got, blocks = lax.optimization_barrier((got, blocks))

    kept = keep_part(place, mine, other, down_weight, *[g.astype(jnp.float32) for g in got])
    kept = kept.astype(jnp.float16).reshape(4, 4, 224, LANES)
    tokens = collect(place, blocks)
    theirs = lax.ppermute(tokens, "xl", SWAP)
    summed, theirs = lax.optimization_barrier((lax.all_to_all(kept, ("z1", "z0"), 0, 0), theirs))

    merged = merge(place, summed.astype(jnp.float32))
    far = [shift(merged[k].astype(jnp.float16), FAR, k).astype(jnp.float32) for k in range(1, 4)]
    gate_grad, up_grad = final([merged[0]] + far, gate_pre, up_pre)

    begun = weight_part(place, tokens, mine, other, hid)
    weight_grad = weight_part(place, theirs, mine, other, hid, begun)
    return (gate_grad, up_grad, weight_grad)


def solution(mesh):
    bits = Mesh(np.asarray(mesh.devices).reshape((2,) * 9), DP + TENSOR)
    return jax.shard_map(
        shards,
        mesh=bits,
        in_specs=(P(DP, TENSOR), P(DP, TENSOR), P(TENSOR, DP), P(TENSOR, DP)),
        out_specs=(P(DP, TENSOR), P(DP, TENSOR), P(TENSOR, DP)),
        check_vma=False,
    )
```

```python
import functools

import jax
import jax.numpy as jnp
import numpy as np
from jax import lax
from jax.experimental import pallas as pl
from jax.experimental.pallas import tpu as pltpu
from jax.sharding import Mesh, PartitionSpec as P

Z = ("z3", "z2", "z1", "z0")
FAR = Z[:2]
DP = ("xl",) + Z
YX = ("y1", "y0", "xh")
TENSOR = YX + ("c",)
SWAP = [(0, 1), (1, 0)]
LANES = 128
VMEM_BYTES = 32 * 1024 * 1024
whole = pl.BlockSpec(memory_space=pltpu.VMEM)
scalars = pl.BlockSpec(memory_space=pltpu.SMEM)


def pack(block):
    tail = block[:, 3 * LANES :]
    packed = tail[0:16]
    for k in range(1, 4):
        packed += pltpu.roll(tail[16 * k : 16 * k + 16], 32 * k, 1)
    return jnp.concatenate([block[:, LANES * k : LANES * (k + 1)] for k in range(3)] + [packed], axis=0)


def encode(packed):
    top = jnp.max(jnp.max(jnp.abs(packed), axis=0, keepdims=True), axis=1, keepdims=True)
    exponent = jnp.floor(jnp.log2(jnp.maximum(top, 1e-37)))
    scaled = packed * jnp.exp2(-exponent)
    return jnp.concatenate([scaled, jnp.broadcast_to(exponent, (16, LANES))], axis=0)


def decode(coded):
    return coded[:208] * jnp.exp2(coded[208:209])


def times(rows, weight):
    return lax.dot_general(rows, weight, (((1,), (1,)), ((), ())), preferred_element_type=jnp.float32)


def send_kernel(place_ref, rows_ref, weight_ref, out_ref, padded):
    hid = weight_ref.shape[0]
    padded[hid:] = jnp.zeros_like(padded[hid:])
    padded[:hid] = weight_ref[...]
    rows = rows_ref[pl.ds((1 - place_ref[0]) * 4, 4)].reshape(512, rows_ref.shape[2])
    product = times(rows, padded[...])
    for far in range(4):
        for half in range(2):
            start = far * 128 + half * 64
            out_ref[half, far] = encode(pack(product[start : start + 64]))


def send_part(place, rows, weight):
    return pl.pallas_call(
        send_kernel,
        out_shape=jax.ShapeDtypeStruct((2, 4, 224, LANES), jnp.float32),
        in_specs=[scalars] + [whole] * 2,
        out_specs=whole,
        scratch_shapes=[pltpu.VMEM((512, weight.shape[1]), weight.dtype)],
        compiler_params=pltpu.CompilerParams(vmem_limit_bytes=VMEM_BYTES),
        cost_estimate=pl.CostEstimate(flops=2 * 512 * 512 * 512, bytes_accessed=2 << 20, transcendentals=0),
        name="send_part",
    )(place, rows, weight)


def keep_kernel(place_ref, mine_ref, other_ref, weight_ref, got_mine_ref, got_other_ref, *refs):
    own_ref, up1_ref, down1_ref, up2_ref, down2_ref, padded = refs
    hid = weight_ref.shape[0]
    padded[hid:] = jnp.zeros_like(padded[hid:])
    padded[:hid] = weight_ref[...]
    xl, c, low = place_ref[0], place_ref[1], lax.rem(place_ref[3], 4)
    products = {}
    for own_core in (True, False):
        ref, got_ref = (mine_ref, got_mine_ref) if own_core else (other_ref, got_other_ref)
        rows = ref[pl.ds(xl * 4, 4)].reshape(512, ref.shape[2])
        product = times(rows, padded[...])
        core = c if own_core else 1 - c
        for half in range(2):
            ahead = lax.rem(core * 2 + half - low + 4, 4)
            for far in range(4):
                start = far * 128 + half * 64
                products[own_core, half, far] = pack(product[start : start + 64]) + decode(got_ref[half, far])

            @pl.when(ahead == 0)
            def _(own_core=own_core, half=half):
                for far in range(4):
                    own_ref[far] = products[own_core, half, far]

            @pl.when(ahead == 1)
            def _(own_core=own_core, half=half):
                for far in range(4):
                    up1_ref[far] = encode(products[own_core, half, far])

            @pl.when(ahead == 2)
            def _(own_core=own_core, half=half):
                for far in range(4):
                    out_ref = up2_ref if far < 2 else down2_ref
                    out_ref[far % 2] = encode(products[own_core, half, far])

            @pl.when(ahead == 3)
            def _(own_core=own_core, half=half):
                for far in range(4):
                    down1_ref[far] = encode(products[own_core, half, far])


def keep_part(place, mine, other, weight, got_mine, got_other):
    shapes = [(4, 208, LANES), (4, 224, LANES), (4, 224, LANES), (2, 224, LANES), (2, 224, LANES)]
    return pl.pallas_call(
        keep_kernel,
        out_shape=tuple(jax.ShapeDtypeStruct(s, jnp.float32) for s in shapes),
        in_specs=[scalars] + [whole] * 5,
        out_specs=(whole,) * 5,
        scratch_shapes=[pltpu.VMEM((512, weight.shape[1]), weight.dtype)],
        compiler_params=pltpu.CompilerParams(vmem_limit_bytes=VMEM_BYTES),
        cost_estimate=pl.CostEstimate(flops=2 * 1024 * 512 * 512, bytes_accessed=4 << 20, transcendentals=0),
        name="keep_part",
    )(place, mine, other, weight, got_mine, got_other)


def merge_kernel(place_ref, own_ref, up1_ref, down1_ref, up2_ref, down2_ref, total_ref, *out_refs):
    for far in range(4):
        twice_ref = up2_ref if far < 2 else down2_ref
        vals = own_ref[far] + decode(up1_ref[far]) + decode(down1_ref[far]) + decode(twice_ref[far % 2])
        ahead = lax.rem(far - place_ref[2] + 4, 4)

        @pl.when(ahead == 0)
        def _(vals=vals):
            total_ref[...] = vals

        for k in range(1, 4):

            @pl.when(ahead == k)
            def _(vals=vals, k=k):
                out_refs[k - 1][...] = encode(vals)


def merge(place, parts):
    return pl.pallas_call(
        merge_kernel,
        out_shape=(jax.ShapeDtypeStruct((208, LANES), jnp.float32),)
        + (jax.ShapeDtypeStruct((224, LANES), jnp.float32),) * 3,
        in_specs=[scalars] + [whole] * 5,
        out_specs=(whole,) * 4,
        compiler_params=pltpu.CompilerParams(vmem_limit_bytes=VMEM_BYTES),
        cost_estimate=pl.CostEstimate(flops=1 << 20, bytes_accessed=1 << 20, transcendentals=0),
        name="merge_parts",
    )(place, *parts)


def final_kernel(own_ref, a_ref, b_ref, d_ref, gate_ref, up_ref, gate_grad_ref, up_grad_ref):
    packed = own_ref[...] + decode(a_ref[...]) + decode(b_ref[...]) + decode(d_ref[...])
    tail = packed[192:208]
    tails = jnp.concatenate([tail] + [pltpu.roll(tail, LANES - 32 * k, 1) for k in range(1, 4)], axis=0)
    width = gate_ref.shape[1]
    for k in range(4):
        cols = slice(LANES * k, min(LANES * (k + 1), width))
        grad = packed[64 * k : 64 * k + 64] if k < 3 else tails[:, : width - 3 * LANES]
        gate = gate_ref[:, cols].astype(jnp.float32)
        up = up_ref[:, cols].astype(jnp.float32)
        s = jax.nn.sigmoid(gate)
        gate_grad_ref[:, cols] = (grad * up * s * (1.0 + gate * (1.0 - s))).astype(gate_grad_ref.dtype)
        up_grad_ref[:, cols] = (grad * (gate * s)).astype(up_grad_ref.dtype)


def final(parts, gate_pre, up_pre):
    return pl.pallas_call(
        final_kernel,
        out_shape=(jax.ShapeDtypeStruct(gate_pre.shape, gate_pre.dtype),) * 2,
        in_specs=[whole] * 6,
        out_specs=(whole, whole),
        compiler_params=pltpu.CompilerParams(vmem_limit_bytes=VMEM_BYTES),
        cost_estimate=pl.CostEstimate(flops=1, bytes_accessed=1, transcendentals=0),
        name="finish_grads",
    )(*parts, gate_pre, up_pre)


def weight_kernel(place_ref, own_ref, partner_ref, mine_ref, other_ref, out_ref):
    xl, c = place_ref[0], place_ref[1]
    total = None
    for hidden_ref, owner in ((own_ref, xl), (partner_ref, 1 - xl)):
        for ref, core in ((mine_ref, c), (other_ref, 1 - c)):
            rows = ref[pl.ds(owner * 4, 4)].reshape(512, ref.shape[2])
            tokens = jnp.concatenate([hidden_ref[far, core] for far in range(4)], axis=1)
            product = jnp.dot(tokens, rows, preferred_element_type=jnp.float32)
            total = product if total is None else total + product
    out_ref[...] = total * 2048 ** (-0.5)


def weight_part(place, own, partner, mine, other):
    return pl.pallas_call(
        weight_kernel,
        out_shape=jax.ShapeDtypeStruct((own.shape[2], mine.shape[2]), jnp.float32),
        in_specs=[scalars] + [whole] * 4,
        out_specs=whole,
        compiler_params=pltpu.CompilerParams(vmem_limit_bytes=VMEM_BYTES),
        cost_estimate=pl.CostEstimate(flops=2 * 2048 * 512 * 512, bytes_accessed=5 << 20, transcendentals=0),
        name="weight_grad",
    )(place, own, partner, mine, other)


def shift(array, axes, step):
    size = 2 ** len(axes)
    return lax.ppermute(array, axes, [(i, (i + step) % size) for i in range(size)])


def shards(gate_pre, up_pre, out_grad, down_weight):
    place = jnp.stack([lax.axis_index("xl"), lax.axis_index("c"), lax.axis_index(FAR), lax.axis_index(Z)]).astype(jnp.int32)
    hid = gate_pre.shape[1]
    gate_vals = gate_pre.astype(jnp.float32)
    hidden = (gate_vals * jax.nn.sigmoid(gate_vals) * up_pre.astype(jnp.float32)).astype(jnp.bfloat16)

    mine = lax.all_to_all(jnp.broadcast_to(out_grad[None], (8,) + out_grad.shape), YX, 0, 0)
    other = lax.ppermute(mine, "c", SWAP)

    sent = [send_part(place, rows, down_weight).astype(jnp.float16) for rows in (mine, other)]
    sent, hidden = lax.optimization_barrier((sent, hidden))
    got = [lax.ppermute(s, "xl", SWAP) for s in sent]
    tokens = lax.all_gather(hidden, Z, axis=0, tiled=True)
    got, tokens = lax.optimization_barrier((got, tokens))
    tokens = tokens.reshape(4, 2, 128, hid).transpose(0, 1, 3, 2)
    theirs = lax.ppermute(tokens, "xl", SWAP)

    kept = keep_part(place, mine, other, down_weight, *[g.astype(jnp.float32) for g in got])
    halves = [k.astype(jnp.float16) for k in kept[1:]]
    near = [shift(h, Z, step) for h, step in zip(halves, (1, -1, 2, -2), strict=True)]
    near, theirs = lax.optimization_barrier((near, theirs))
    merged = merge(place, [kept[0]] + [n.astype(jnp.float32) for n in near])
    far = [shift(merged[k].astype(jnp.float16), FAR, k).astype(jnp.float32) for k in range(1, 4)]
    gate_grad, up_grad = final([merged[0]] + far, gate_pre, up_pre)

    weight_grad = weight_part(place, tokens, theirs, mine, other)
    return (gate_grad, up_grad, weight_grad)


def solution(mesh):
    bits = Mesh(np.asarray(mesh.devices).reshape((2,) * 9), DP + TENSOR)
    return jax.shard_map(
        shards,
        mesh=bits,
        in_specs=(P(DP, TENSOR), P(DP, TENSOR), P(TENSOR, DP), P(TENSOR, DP)),
        out_specs=(P(DP, TENSOR), P(DP, TENSOR), P(TENSOR, DP)),
        check_vma=False,
    )
```

```python
import functools

import jax
import jax.numpy as jnp
import numpy as np
from jax import lax
from jax.experimental import pallas as pl
from jax.experimental.pallas import tpu as pltpu
from jax.sharding import Mesh, PartitionSpec as P

Z = ("z3", "z2", "z1", "z0")
FAR = Z[:2]
DP = ("xl",) + Z
YX = ("y1", "y0", "xh")
TENSOR = YX + ("c",)
SWAP = [(0, 1), (1, 0)]
TURN = [(0, 0), (1, 2), (2, 1), (3, 3)]
LANES = 128
VMEM_BYTES = 32 * 1024 * 1024
whole = pl.BlockSpec(memory_space=pltpu.VMEM)
scalars = pl.BlockSpec(memory_space=pltpu.SMEM)


def pack(block):
    tail = block[:, 3 * LANES :]
    packed = tail[0:16]
    for k in range(1, 4):
        packed += pltpu.roll(tail[16 * k : 16 * k + 16], 32 * k, 1)
    return jnp.concatenate([block[:, LANES * k : LANES * (k + 1)] for k in range(3)] + [packed], axis=0)


def encode(packed):
    top = jnp.max(jnp.max(jnp.abs(packed), axis=0, keepdims=True), axis=1, keepdims=True)
    exponent = jnp.floor(jnp.log2(jnp.maximum(top, 1e-37)))
    scaled = packed * jnp.exp2(-exponent)
    return jnp.concatenate([scaled, jnp.broadcast_to(exponent, (16, LANES))], axis=0)


def decode(coded):
    return coded[:208] * jnp.exp2(coded[208:209])


def times(rows, weight):
    return lax.dot_general(rows, weight, (((1,), (1,)), ((), ())), preferred_element_type=jnp.float32)


def keep_kernel(place_ref, grad_ref, own_weight_ref, their_weight_ref, *refs):
    own_ref, up1_ref, down1_ref, up2_ref, down2_ref, padded = refs
    hid, feats = own_weight_ref.shape
    xl, low = place_ref[0], place_ref[1]
    padded[:, hid:] = jnp.zeros_like(padded[:, hid:])
    padded[xl, :hid] = own_weight_ref[...]
    padded[1 - xl, :hid] = their_weight_ref[...]
    for y1 in range(2):
        product = sum(times(grad_ref[y1 * 4 : y1 * 4 + 4, k].reshape(512, feats), padded[k]) for k in range(2))
        for half in range(2):
            ahead = lax.rem(y1 * 2 + half - low + 4, 4)
            vals = [pack(product[far * 128 + half * 64 :][:64]) for far in range(4)]

            @pl.when(ahead == 0)
            def _(vals=vals):
                for far in range(4):
                    own_ref[far] = vals[far]

            @pl.when(ahead == 1)
            def _(vals=vals):
                for far in range(4):
                    up1_ref[far] = encode(vals[far])

            @pl.when(ahead == 2)
            def _(vals=vals):
                for far in range(4):
                    out_ref = up2_ref if far < 2 else down2_ref
                    out_ref[far % 2] = encode(vals[far])

            @pl.when(ahead == 3)
            def _(vals=vals):
                for far in range(4):
                    down1_ref[far] = encode(vals[far])


def keep_part(place, grad, own_weight, their_weight):
    shapes = [(4, 208, LANES), (4, 224, LANES), (4, 224, LANES), (2, 224, LANES), (2, 224, LANES)]
    return pl.pallas_call(
        keep_kernel,
        out_shape=tuple(jax.ShapeDtypeStruct(s, jnp.float32) for s in shapes),
        in_specs=[scalars] + [whole] * 3,
        out_specs=(whole,) * 5,
        scratch_shapes=[pltpu.VMEM((2, 512, own_weight.shape[1]), own_weight.dtype)],
        compiler_params=pltpu.CompilerParams(vmem_limit_bytes=VMEM_BYTES),
        cost_estimate=pl.CostEstimate(flops=2 * 1024 * 1024 * 512, bytes_accessed=4 << 20, transcendentals=0),
        name="keep_part",
    )(place, grad, own_weight, their_weight)


def merge_kernel(place_ref, own_ref, up1_ref, down1_ref, up2_ref, down2_ref, *out_refs):
    for far in range(4):
        twice_ref = up2_ref if far < 2 else down2_ref
        vals = own_ref[far] + decode(up1_ref[far]) + decode(down1_ref[far]) + decode(twice_ref[far % 2])
        ahead = lax.rem(far - place_ref[2] + 4, 4)
        for k in range(4):

            @pl.when(ahead == k)
            def _(vals=vals, k=k):
                out_refs[k][...] = encode(vals)


def merge(place, parts):
    return pl.pallas_call(
        merge_kernel,
        out_shape=(jax.ShapeDtypeStruct((224, LANES), jnp.float32),) * 4,
        in_specs=[scalars] + [whole] * 5,
        out_specs=(whole,) * 4,
        compiler_params=pltpu.CompilerParams(vmem_limit_bytes=VMEM_BYTES),
        cost_estimate=pl.CostEstimate(flops=1 << 20, bytes_accessed=1 << 20, transcendentals=0),
        name="merge_parts",
    )(place, *parts)


def final_kernel(a_ref, b_ref, d_ref, e_ref, gate_ref, up_ref, gate_grad_ref, up_grad_ref):
    packed = decode(a_ref[...]) + decode(b_ref[...]) + decode(d_ref[...]) + decode(e_ref[...])
    tail = packed[192:208]
    tails = jnp.concatenate([tail] + [pltpu.roll(tail, LANES - 32 * k, 1) for k in range(1, 4)], axis=0)
    width = gate_ref.shape[1]
    for k in range(4):
        cols = slice(LANES * k, min(LANES * (k + 1), width))
        grad = packed[64 * k : 64 * k + 64] if k < 3 else tails[:, : width - 3 * LANES]
        gate = gate_ref[:, cols].astype(jnp.float32)
        up = up_ref[:, cols].astype(jnp.float32)
        s = jax.nn.sigmoid(gate)
        gate_grad_ref[:, cols] = (grad * up * s * (1.0 + gate * (1.0 - s))).astype(gate_grad_ref.dtype)
        up_grad_ref[:, cols] = (grad * (gate * s)).astype(up_grad_ref.dtype)


def final(parts, gate_pre, up_pre):
    return pl.pallas_call(
        final_kernel,
        out_shape=(jax.ShapeDtypeStruct(gate_pre.shape, gate_pre.dtype),) * 2,
        in_specs=[whole] * 6,
        out_specs=(whole, whole),
        compiler_params=pltpu.CompilerParams(vmem_limit_bytes=VMEM_BYTES),
        cost_estimate=pl.CostEstimate(flops=1, bytes_accessed=1, transcendentals=0),
        name="finish_grads",
    )(*parts, gate_pre, up_pre)


def weight_kernel(place_ref, hidden_ref, grad_ref, own_ref, their_ref):
    xl = place_ref[0]
    feats = own_ref.shape[1]
    tokens = [hidden_ref[:, y1].reshape(512, hidden_ref.shape[3]) for y1 in range(2)]
    for out_ref, k in ((their_ref, 1 - xl), (own_ref, xl)):
        out_ref[...] = sum(
            lax.dot_general(
                tokens[y1],
                grad_ref[y1 * 4 : y1 * 4 + 4, k].reshape(512, feats),
                (((0,), (0,)), ((), ())),
                preferred_element_type=jnp.float32,
            )
            for y1 in range(2)
        )


def weight_part(place, hidden, grad):
    return pl.pallas_call(
        weight_kernel,
        out_shape=(jax.ShapeDtypeStruct((hidden.shape[3], grad.shape[3]), jnp.float32),) * 2,
        in_specs=[scalars] + [whole] * 2,
        out_specs=(whole, whole),
        compiler_params=pltpu.CompilerParams(vmem_limit_bytes=VMEM_BYTES),
        cost_estimate=pl.CostEstimate(flops=2 * 2048 * 512 * 512, bytes_accessed=5 << 20, transcendentals=0),
        name="weight_part",
    )(place, hidden, grad)


def shift(array, axes, step):
    size = 2 ** len(axes)
    return lax.ppermute(array, axes, [(i, (i + step) % size) for i in range(size)])


def to_owner(array, step):
    pairs = [
        (a * 8 + far * 2 + b, b * 8 + (far + step) % 4 * 2 + a) for a in range(2) for far in range(4) for b in range(2)
    ]
    return lax.ppermute(array, ("xl",) + FAR + ("z1",), pairs)


def shards(gate_pre, up_pre, out_grad, down_weight):
    place = jnp.stack([lax.axis_index("xl"), lax.axis_index(Z[2:]), lax.axis_index(FAR)]).astype(jnp.int32)
    hid, feats = down_weight.shape
    gate_vals = gate_pre.astype(jnp.float32)
    hidden = (gate_vals * jax.nn.sigmoid(gate_vals) * up_pre.astype(jnp.float32)).astype(jnp.bfloat16)

    hidden = lax.ppermute(hidden, ("xl", "z1"), TURN)
    turned = lax.ppermute(out_grad, ("xl", "c"), TURN)
    their_weight = lax.ppermute(down_weight, "xl", SWAP)
    hidden, turned = lax.optimization_barrier((hidden, turned))
    grad = lax.all_to_all(jnp.broadcast_to(turned[None], (16,) + turned.shape), TENSOR, 0, 0)
    tokens = lax.all_gather(hidden, Z, axis=0, tiled=True)
    grad, tokens, their_weight = lax.optimization_barrier((grad, tokens, their_weight))
    grad = grad.reshape(8, 2, 128, feats)

    kept = keep_part(place, grad, down_weight, their_weight)
    halves = [k.astype(jnp.float16) for k in kept[1:]]
    near = [shift(h, Z, step) for h, step in zip(halves, (1, -1, 2, -2), strict=True)]
    own, theirs = weight_part(place, tokens.reshape(4, 2, 128, hid), grad)
    near, theirs = lax.optimization_barrier((near, theirs))
    merged = merge(place, [kept[0]] + [n.astype(jnp.float32) for n in near])
    got = lax.ppermute(theirs, "xl", SWAP)
    far = [to_owner(m.astype(jnp.float16), k).astype(jnp.float32) for k, m in enumerate(merged)]
    gate_grad, up_grad = final(far, gate_pre, up_pre)
    weight_grad = (own + got) * 2048 ** (-0.5)
    return (gate_grad, up_grad, weight_grad)


def solution(mesh):
    bits = Mesh(np.asarray(mesh.devices).reshape((2,) * 9), DP + TENSOR)
    return jax.shard_map(
        shards,
        mesh=bits,
        in_specs=(P(DP, TENSOR), P(DP, TENSOR), P(TENSOR, DP), P(TENSOR, DP)),
        out_specs=(P(DP, TENSOR), P(DP, TENSOR), P(TENSOR, DP)),
        check_vma=False,
    )
```

```python
import functools

import jax
import jax.numpy as jnp
import numpy as np
from jax import lax
from jax.experimental import pallas as pl
from jax.experimental.pallas import tpu as pltpu
from jax.sharding import Mesh, PartitionSpec as P

Z = ("z3", "z2", "z1", "z0")
FAR = Z[:2]
DP = ("xl",) + Z
YX = ("y1", "y0", "xh")
TENSOR = YX + ("c",)
SWAP = [(0, 1), (1, 0)]
TURN = [(0, 0), (1, 2), (2, 1), (3, 3)]
LANES = 128
VMEM_BYTES = 32 * 1024 * 1024
whole = pl.BlockSpec(memory_space=pltpu.VMEM)
scalars = pl.BlockSpec(memory_space=pltpu.SMEM)


def pack(block):
    tail = block[:, 3 * LANES :]
    packed = tail[0:16]
    for k in range(1, 4):
        packed += pltpu.roll(tail[16 * k : 16 * k + 16], 32 * k, 1)
    return jnp.concatenate([block[:, LANES * k : LANES * (k + 1)] for k in range(3)] + [packed], axis=0)


def encode(packed):
    top = jnp.max(jnp.max(jnp.abs(packed), axis=0, keepdims=True), axis=1, keepdims=True)
    exponent = jnp.floor(jnp.log2(jnp.maximum(top, 1e-37)))
    scaled = packed * jnp.exp2(-exponent)
    return jnp.concatenate([scaled, jnp.broadcast_to(exponent, (16, LANES))], axis=0)


def decode(coded):
    return coded[:208] * jnp.exp2(coded[208:209])


def times(rows, weight):
    return lax.dot_general(rows, weight, (((1,), (1,)), ((), ())), preferred_element_type=jnp.float32)


def keep_kernel(place_ref, grad_ref, own_weight_ref, their_weight_ref, *refs):
    own_ref, up1_ref, down1_ref, up2_ref, down2_ref, padded = refs
    hid = own_weight_ref.shape[0]
    xl, low = place_ref[0], place_ref[1]
    padded[:, hid:] = jnp.zeros_like(padded[:, hid:])
    padded[xl, :hid] = own_weight_ref[...]
    padded[1 - xl, :hid] = their_weight_ref[...]
    for y1 in range(2):
        product = sum(times(grad_ref[k, y1], padded[k]) for k in range(2))
        for core in range(2):
            ahead = lax.rem(core * 2 + y1 - low + 4, 4)
            vals = [pack(product[far * 128 + core * 64 :][:64]) for far in range(4)]

            @pl.when(ahead == 0)
            def _(vals=vals):
                for far in range(4):
                    own_ref[far] = vals[far]

            @pl.when(ahead == 1)
            def _(vals=vals):
                for far in range(4):
                    up1_ref[far] = encode(vals[far])

            @pl.when(ahead == 2)
            def _(vals=vals):
                for far in range(4):
                    out_ref = up2_ref if far < 2 else down2_ref
                    out_ref[far % 2] = encode(vals[far])

            @pl.when(ahead == 3)
            def _(vals=vals):
                for far in range(4):
                    down1_ref[far] = encode(vals[far])


def keep_part(place, grad, own_weight, their_weight):
    shapes = [(4, 208, LANES), (4, 224, LANES), (4, 224, LANES), (2, 224, LANES), (2, 224, LANES)]
    return pl.pallas_call(
        keep_kernel,
        out_shape=tuple(jax.ShapeDtypeStruct(s, jnp.float32) for s in shapes),
        in_specs=[scalars] + [whole] * 3,
        out_specs=(whole,) * 5,
        scratch_shapes=[pltpu.VMEM((2, 512, own_weight.shape[1]), own_weight.dtype)],
        compiler_params=pltpu.CompilerParams(vmem_limit_bytes=VMEM_BYTES),
        cost_estimate=pl.CostEstimate(flops=2 * 1024 * 1024 * 512, bytes_accessed=4 << 20, transcendentals=0),
        name="keep_part",
    )(place, grad, own_weight, their_weight)


def merge_kernel(place_ref, own_ref, up1_ref, down1_ref, up2_ref, down2_ref, *out_refs):
    for far in range(4):
        twice_ref = up2_ref if far < 2 else down2_ref
        vals = own_ref[far] + decode(up1_ref[far]) + decode(down1_ref[far]) + decode(twice_ref[far % 2])
        ahead = lax.rem(far - place_ref[2] + 4, 4)
        for k in range(4):

            @pl.when(ahead == k)
            def _(vals=vals, k=k):
                out_refs[k][...] = encode(vals)


def merge(place, parts):
    return pl.pallas_call(
        merge_kernel,
        out_shape=(jax.ShapeDtypeStruct((224, LANES), jnp.float32),) * 4,
        in_specs=[scalars] + [whole] * 5,
        out_specs=(whole,) * 4,
        compiler_params=pltpu.CompilerParams(vmem_limit_bytes=VMEM_BYTES),
        cost_estimate=pl.CostEstimate(flops=1 << 20, bytes_accessed=1 << 20, transcendentals=0),
        name="merge_parts",
    )(place, *parts)


def final_kernel(a_ref, b_ref, d_ref, e_ref, gate_ref, up_ref, gate_grad_ref, up_grad_ref):
    packed = decode(a_ref[...]) + decode(b_ref[...]) + decode(d_ref[...]) + decode(e_ref[...])
    tail = packed[192:208]
    tails = jnp.concatenate([tail] + [pltpu.roll(tail, LANES - 32 * k, 1) for k in range(1, 4)], axis=0)
    width = gate_ref.shape[1]
    for k in range(4):
        cols = slice(LANES * k, min(LANES * (k + 1), width))
        grad = packed[64 * k : 64 * k + 64] if k < 3 else tails[:, : width - 3 * LANES]
        gate = gate_ref[:, cols].astype(jnp.float32)
        up = up_ref[:, cols].astype(jnp.float32)
        s = jax.nn.sigmoid(gate)
        gate_grad_ref[:, cols] = (grad * up * s * (1.0 + gate * (1.0 - s))).astype(gate_grad_ref.dtype)
        up_grad_ref[:, cols] = (grad * (gate * s)).astype(up_grad_ref.dtype)


def final(parts, gate_pre, up_pre):
    return pl.pallas_call(
        final_kernel,
        out_shape=(jax.ShapeDtypeStruct(gate_pre.shape, gate_pre.dtype),) * 2,
        in_specs=[whole] * 6,
        out_specs=(whole, whole),
        compiler_params=pltpu.CompilerParams(vmem_limit_bytes=VMEM_BYTES),
        cost_estimate=pl.CostEstimate(flops=1, bytes_accessed=1, transcendentals=0),
        name="finish_grads",
    )(*parts, gate_pre, up_pre)


def weight_kernel(place_ref, hidden_ref, grad_ref, own_ref, their_ref):
    xl = place_ref[0]
    tokens = [hidden_ref[:, y1].reshape(512, hidden_ref.shape[3]) for y1 in range(2)]
    for out_ref, k in ((their_ref, 1 - xl), (own_ref, xl)):
        out_ref[...] = sum(
            lax.dot_general(
                tokens[y1],
                grad_ref[k, y1],
                (((0,), (0,)), ((), ())),
                preferred_element_type=jnp.float32,
            )
            for y1 in range(2)
        )


def weight_part(place, hidden, grad):
    return pl.pallas_call(
        weight_kernel,
        out_shape=(jax.ShapeDtypeStruct((hidden.shape[3], grad.shape[3]), jnp.float32),) * 2,
        in_specs=[scalars] + [whole] * 2,
        out_specs=(whole, whole),
        compiler_params=pltpu.CompilerParams(vmem_limit_bytes=VMEM_BYTES),
        cost_estimate=pl.CostEstimate(flops=2 * 2048 * 512 * 512, bytes_accessed=5 << 20, transcendentals=0),
        name="weight_part",
    )(place, hidden, grad)


def shift(array, axes, step):
    size = 2 ** len(axes)
    return lax.ppermute(array, axes, [(i, (i + step) % size) for i in range(size)])


def to_owner(array, step):
    pairs = [
        (a * 8 + far * 2 + b, b * 8 + (far + step) % 4 * 2 + a) for a in range(2) for far in range(4) for b in range(2)
    ]
    return lax.ppermute(array, ("xl",) + FAR + ("z0",), pairs)


def shards(gate_pre, up_pre, out_grad, down_weight):
    place = jnp.stack([lax.axis_index("xl"), lax.axis_index(Z[2:]), lax.axis_index(FAR)]).astype(jnp.int32)
    hid, feats = down_weight.shape
    gate_vals = gate_pre.astype(jnp.float32)
    hidden = (gate_vals * jax.nn.sigmoid(gate_vals) * up_pre.astype(jnp.float32)).astype(jnp.bfloat16)

    hidden = lax.ppermute(hidden, ("xl", "z0"), TURN)
    their_weight = lax.ppermute(down_weight, "xl", SWAP)
    copies = jnp.broadcast_to(out_grad.reshape(2, 1, 64, feats), (2, 16, 64, feats)).reshape(32, 64, feats)
    grad = lax.all_to_all(copies, ("xl",) + TENSOR, 0, 0)
    tokens = lax.all_gather(hidden, Z, axis=0, tiled=True)
    grad, tokens, their_weight = lax.optimization_barrier((grad, tokens, their_weight))
    grad = grad.reshape(2, 2, 512, feats)

    kept = keep_part(place, grad, down_weight, their_weight)
    halves = [k.astype(jnp.float16) for k in kept[1:]]
    near = [shift(h, Z, step) for h, step in zip(halves, (1, -1, 2, -2), strict=True)]
    own, theirs = weight_part(place, tokens.reshape(8, 2, 64, hid), grad)
    near, theirs = lax.optimization_barrier((near, theirs))
    merged = merge(place, [kept[0]] + [n.astype(jnp.float32) for n in near])
    got = lax.ppermute(theirs, "xl", SWAP)
    far = [to_owner(m.astype(jnp.float16), k) for k, m in enumerate(merged)]
    weight_grad = (own + got) * 2048 ** (-0.5)
    far, weight_grad = lax.optimization_barrier((far, weight_grad))
    gate_grad, up_grad = final([f.astype(jnp.float32) for f in far], gate_pre, up_pre)
    return (gate_grad, up_grad, weight_grad)


def solution(mesh):
    bits = Mesh(np.asarray(mesh.devices).reshape((2,) * 9), DP + TENSOR)
    return jax.shard_map(
        shards,
        mesh=bits,
        in_specs=(P(DP, TENSOR), P(DP, TENSOR), P(TENSOR, DP), P(TENSOR, DP)),
        out_specs=(P(DP, TENSOR), P(DP, TENSOR), P(TENSOR, DP)),
        check_vma=False,
    )
```

```python
import functools

import jax
import jax.numpy as jnp
import numpy as np
from jax import lax
from jax.experimental import pallas as pl
from jax.experimental.pallas import tpu as pltpu
from jax.sharding import Mesh, PartitionSpec as P

Z = ("z3", "z2", "z1", "z0")
FAR = Z[:2]
DP = ("xl",) + Z
YX = ("y1", "y0", "xh")
TENSOR = YX + ("c",)
SWAP = [(0, 1), (1, 0)]
TURN = [(0, 0), (1, 2), (2, 1), (3, 3)]
LANES = 128
VMEM_BYTES = 16 * 1024 * 1024
whole = pl.BlockSpec(memory_space=pltpu.VMEM)
scalars = pl.BlockSpec(memory_space=pltpu.SMEM)


def pack(block):
    tail = block[:, 3 * LANES :]
    packed = tail[0:16]
    for k in range(1, 4):
        packed += pltpu.roll(tail[16 * k : 16 * k + 16], 32 * k, 1)
    return jnp.concatenate([block[:, LANES * k : LANES * (k + 1)] for k in range(3)] + [packed], axis=0)


def encode(packed):
    top = jnp.max(jnp.max(jnp.abs(packed), axis=0, keepdims=True), axis=1, keepdims=True)
    exponent = jnp.floor(jnp.log2(jnp.maximum(top, 1e-37)))
    scaled = packed * jnp.exp2(-exponent)
    return jnp.concatenate([scaled, jnp.broadcast_to(exponent, (16, LANES))], axis=0)


def decode(coded):
    return coded[:208] * jnp.exp2(coded[208:209])


def times(rows, weight):
    return lax.dot_general(rows, weight, (((1,), (1,)), ((), ())), preferred_element_type=jnp.float32)


def keep_kernel(for_others, place_ref, grad_ref, own_weight_ref, their_weight_ref, tokens_ref, *refs):
    del tokens_ref
    out_refs, padded = refs[:-1], refs[-1]
    hid, feats = own_weight_ref.shape
    xl, low = place_ref[0], place_ref[1]
    padded[:, hid:] = jnp.zeros_like(padded[:, hid:])
    padded[xl, :hid] = own_weight_ref[...]
    padded[1 - xl, :hid] = their_weight_ref[...]
    for ahead in (1, 3, 2) if for_others else (0,):
        place = lax.rem(low + ahead, 4)
        y1, core = lax.rem(place, 2), place // 2
        product = sum(times(grad_ref[k, y1, :, core].reshape(256, feats), padded[k]) for k in range(2))
        for far in range(4):
            vals = pack(product[64 * far : 64 * far + 64])
            if ahead == 0:
                out_refs[0][far] = vals
            elif ahead == 1:
                out_refs[0][far] = encode(vals)
            elif ahead == 3:
                out_refs[1][far] = encode(vals)
            else:
                out_refs[2 + far // 2][far % 2] = encode(vals)


def keep_part(for_others, place, grad, own_weight, their_weight, tokens):
    shapes = [(4, 224, LANES), (4, 224, LANES), (2, 224, LANES), (2, 224, LANES)] if for_others else [(4, 208, LANES)]
    return pl.pallas_call(
        functools.partial(keep_kernel, for_others),
        out_shape=tuple(jax.ShapeDtypeStruct(s, jnp.float32) for s in shapes),
        in_specs=[scalars] + [whole] * 4,
        out_specs=(whole,) * len(shapes),
        scratch_shapes=[pltpu.VMEM((2, 512, own_weight.shape[1]), own_weight.dtype)],
        compiler_params=pltpu.CompilerParams(vmem_limit_bytes=VMEM_BYTES),
        cost_estimate=pl.CostEstimate(flops=2 * 256 * 1024 * 512, bytes_accessed=3 << 20, transcendentals=0),
        name="keep_others" if for_others else "keep_own",
    )(place, grad, own_weight, their_weight, tokens)


def merge_kernel(place_ref, own_ref, up1_ref, down1_ref, up2_ref, down2_ref, *out_refs):
    for far in range(4):
        twice_ref = up2_ref if far < 2 else down2_ref
        vals = own_ref[far] + decode(up1_ref[far]) + decode(down1_ref[far]) + decode(twice_ref[far % 2])
        ahead = lax.rem(far - place_ref[2] + 4, 4)
        for k in range(4):

            @pl.when(ahead == k)
            def _(vals=vals, k=k):
                out_refs[k][...] = encode(vals)


def merge(place, parts):
    return pl.pallas_call(
        merge_kernel,
        out_shape=(jax.ShapeDtypeStruct((224, LANES), jnp.float32),) * 4,
        in_specs=[scalars] + [whole] * 5,
        out_specs=(whole,) * 4,
        compiler_params=pltpu.CompilerParams(vmem_limit_bytes=VMEM_BYTES),
        cost_estimate=pl.CostEstimate(flops=1 << 20, bytes_accessed=1 << 20, transcendentals=0),
        name="merge_parts",
    )(place, *parts)


def final_kernel(a_ref, b_ref, d_ref, e_ref, gate_ref, up_ref, gate_grad_ref, up_grad_ref):
    packed = decode(a_ref[...]) + decode(b_ref[...]) + decode(d_ref[...]) + decode(e_ref[...])
    tail = packed[192:208]
    tails = jnp.concatenate([tail] + [pltpu.roll(tail, LANES - 32 * k, 1) for k in range(1, 4)], axis=0)
    width = gate_ref.shape[1]
    for k in range(4):
        cols = slice(LANES * k, min(LANES * (k + 1), width))
        grad = packed[64 * k : 64 * k + 64] if k < 3 else tails[:, : width - 3 * LANES]
        gate = gate_ref[:, cols].astype(jnp.float32)
        up = up_ref[:, cols].astype(jnp.float32)
        s = jax.nn.sigmoid(gate)
        gate_grad_ref[:, cols] = (grad * up * s * (1.0 + gate * (1.0 - s))).astype(gate_grad_ref.dtype)
        up_grad_ref[:, cols] = (grad * (gate * s)).astype(up_grad_ref.dtype)


def final(parts, gate_pre, up_pre):
    return pl.pallas_call(
        final_kernel,
        out_shape=(jax.ShapeDtypeStruct(gate_pre.shape, gate_pre.dtype),) * 2,
        in_specs=[whole] * 6,
        out_specs=(whole, whole),
        compiler_params=pltpu.CompilerParams(vmem_limit_bytes=VMEM_BYTES),
        cost_estimate=pl.CostEstimate(flops=1, bytes_accessed=1, transcendentals=0),
        name="finish_grads",
    )(*parts, gate_pre, up_pre)


def weight_kernel(place_ref, hidden_ref, grad_ref, own_ref, their_ref):
    xl = place_ref[0]
    tokens = [hidden_ref[:, y1].reshape(512, hidden_ref.shape[3]) for y1 in range(2)]
    for out_ref, k in ((their_ref, 1 - xl), (own_ref, xl)):
        out_ref[...] = sum(
            lax.dot_general(
                tokens[y1],
                grad_ref[k, y1],
                (((0,), (0,)), ((), ())),
                preferred_element_type=jnp.float32,
            )
            for y1 in range(2)
        )


def weight_part(place, hidden, grad):
    return pl.pallas_call(
        weight_kernel,
        out_shape=(jax.ShapeDtypeStruct((hidden.shape[3], grad.shape[3]), jnp.float32),) * 2,
        in_specs=[scalars] + [whole] * 2,
        out_specs=(whole, whole),
        compiler_params=pltpu.CompilerParams(vmem_limit_bytes=VMEM_BYTES),
        cost_estimate=pl.CostEstimate(flops=2 * 2048 * 512 * 512, bytes_accessed=5 << 20, transcendentals=0),
        name="weight_part",
    )(place, hidden, grad)


def shift(array, axes, step):
    size = 2 ** len(axes)
    return lax.ppermute(array, axes, [(i, (i + step) % size) for i in range(size)])


def to_owner(array, step):
    pairs = [
        (a * 8 + far * 2 + b, b * 8 + (far + step) % 4 * 2 + a) for a in range(2) for far in range(4) for b in range(2)
    ]
    return lax.ppermute(array, ("xl",) + FAR + ("z0",), pairs)


def shards(gate_pre, up_pre, out_grad, down_weight):
    place = jnp.stack([lax.axis_index("xl"), lax.axis_index(Z[2:]), lax.axis_index(FAR)]).astype(jnp.int32)
    hid, feats = down_weight.shape
    gate_vals = gate_pre.astype(jnp.float32)
    hidden = (gate_vals * jax.nn.sigmoid(gate_vals) * up_pre.astype(jnp.float32)).astype(jnp.bfloat16)

    hidden = lax.ppermute(hidden, ("xl", "z0"), TURN)
    their_weight = lax.ppermute(down_weight, "xl", SWAP)
    copies = jnp.broadcast_to(out_grad.reshape(2, 1, 64, feats), (2, 16, 64, feats)).reshape(32, 64, feats)
    grad = lax.all_to_all(copies, ("xl",) + TENSOR, 0, 0)
    tokens = lax.all_gather(hidden, Z, axis=0, tiled=True)
    grad, tokens, their_weight = lax.optimization_barrier((grad, tokens, their_weight))
    blocks = grad.reshape(2, 2, 4, 2, 64, feats)

    halves = [k.astype(jnp.float16) for k in keep_part(True, place, blocks, down_weight, their_weight, tokens)]
    near = [shift(h, Z, step) for h, step in zip(halves, (1, -1, 2, -2), strict=True)]
    (kept,) = keep_part(False, place, blocks, down_weight, their_weight, tokens)
    own, theirs = weight_part(place, tokens.reshape(8, 2, 64, hid), grad.reshape(2, 2, 512, feats))
    near, kept, theirs = lax.optimization_barrier((near, kept, theirs))
    merged = merge(place, [kept] + [n.astype(jnp.float32) for n in near])
    got = lax.ppermute(theirs, "xl", SWAP)
    far = [to_owner(merged[k].astype(jnp.float16), k) for k in (2, 1, 3, 0)]
    weight_grad = (own + got) * 2048 ** (-0.5)
    far, weight_grad = lax.optimization_barrier((far, weight_grad))
    gate_grad, up_grad = final([f.astype(jnp.float32) for f in far], gate_pre, up_pre)
    return (gate_grad, up_grad, weight_grad)


def solution(mesh):
    bits = Mesh(np.asarray(mesh.devices).reshape((2,) * 9), DP + TENSOR)
    return jax.shard_map(
        shards,
        mesh=bits,
        in_specs=(P(DP, TENSOR), P(DP, TENSOR), P(TENSOR, DP), P(TENSOR, DP)),
        out_specs=(P(DP, TENSOR), P(DP, TENSOR), P(TENSOR, DP)),
        check_vma=False,
    )
```

```python
import functools

import jax
import jax.numpy as jnp
import numpy as np
from jax import lax
from jax.experimental import pallas as pl
from jax.experimental.pallas import tpu as pltpu
from jax.sharding import Mesh, PartitionSpec as P

Z = ("z3", "z2", "z1", "z0")
FAR = Z[:2]
DP = ("xl",) + Z
YX = ("y1", "y0", "xh")
TENSOR = YX + ("c",)
SWAP = [(0, 1), (1, 0)]
TURN = [(0, 0), (1, 2), (2, 1), (3, 3)]
LANES = 128
VMEM_BYTES = 16 * 1024 * 1024
whole = pl.BlockSpec(memory_space=pltpu.VMEM)
scalars = pl.BlockSpec(memory_space=pltpu.SMEM)


def pack(block):
    tail = block[:, 3 * LANES :]
    packed = tail[0:16]
    for k in range(1, 4):
        packed += pltpu.roll(tail[16 * k : 16 * k + 16], 32 * k, 1)
    return jnp.concatenate([block[:, LANES * k : LANES * (k + 1)] for k in range(3)] + [packed], axis=0)


def encode(packed):
    top = jnp.max(jnp.max(jnp.abs(packed), axis=0, keepdims=True), axis=1, keepdims=True)
    exponent = jnp.floor(jnp.log2(jnp.maximum(top, 1e-37)))
    scaled = packed * jnp.exp2(-exponent)
    return jnp.concatenate([scaled, jnp.broadcast_to(exponent, (16, LANES))], axis=0)


def decode(coded):
    return coded[:208] * jnp.exp2(coded[208:209])


def times(rows, weight):
    return lax.dot_general(rows, weight, (((1,), (1,)), ((), ())), preferred_element_type=jnp.float32)


def keep_kernel(for_others, place_ref, grad_ref, own_weight_ref, their_weight_ref, tokens_ref, *refs):
    del tokens_ref
    out_refs, padded = refs[:-1], refs[-1]
    hid, feats = own_weight_ref.shape
    xl, low = place_ref[0], place_ref[1]
    padded[:, hid:] = jnp.zeros_like(padded[:, hid:])
    padded[xl, :hid] = own_weight_ref[...]
    padded[1 - xl, :hid] = their_weight_ref[...]
    for ahead in (1, 3, 2) if for_others else (0,):
        place = lax.rem(low + ahead, 4)
        y1, core = lax.rem(place, 2), place // 2
        product = sum(times(grad_ref[k, y1, :, core].reshape(256, feats), padded[k]) for k in range(2))
        for far in range(4):
            vals = pack(product[64 * far : 64 * far + 64])
            if ahead == 0:
                out_refs[0][far] = vals
            elif ahead == 1:
                out_refs[0][far] = encode(vals)
            elif ahead == 3:
                out_refs[1][far] = encode(vals)
            else:
                out_refs[2 + far // 2][far % 2] = encode(vals)


def keep_part(for_others, place, grad, own_weight, their_weight, tokens):
    shapes = [(4, 224, LANES), (4, 224, LANES), (2, 224, LANES), (2, 224, LANES)] if for_others else [(4, 208, LANES)]
    return pl.pallas_call(
        functools.partial(keep_kernel, for_others),
        out_shape=tuple(jax.ShapeDtypeStruct(s, jnp.float32) for s in shapes),
        in_specs=[scalars] + [whole] * 4,
        out_specs=(whole,) * len(shapes),
        scratch_shapes=[pltpu.VMEM((2, 512, own_weight.shape[1]), own_weight.dtype)],
        compiler_params=pltpu.CompilerParams(vmem_limit_bytes=VMEM_BYTES),
        cost_estimate=pl.CostEstimate(flops=2 * 256 * 1024 * 512, bytes_accessed=3 << 20, transcendentals=0),
        name="keep_others" if for_others else "keep_own",
    )(place, grad, own_weight, their_weight, tokens)


def merge_kernel(place_ref, own_ref, up1_ref, down1_ref, up2_ref, down2_ref, *out_refs):
    for far in range(4):
        twice_ref = up2_ref if far < 2 else down2_ref
        vals = own_ref[far] + decode(up1_ref[far]) + decode(down1_ref[far]) + decode(twice_ref[far % 2])
        ahead = lax.rem(far - place_ref[2] + 4, 4)
        for k in range(4):

            @pl.when(ahead == k)
            def _(vals=vals, k=k):
                out_refs[k][...] = encode(vals)


def merge(place, parts):
    return pl.pallas_call(
        merge_kernel,
        out_shape=(jax.ShapeDtypeStruct((224, LANES), jnp.float32),) * 4,
        in_specs=[scalars] + [whole] * 5,
        out_specs=(whole,) * 4,
        compiler_params=pltpu.CompilerParams(vmem_limit_bytes=VMEM_BYTES),
        cost_estimate=pl.CostEstimate(flops=1 << 20, bytes_accessed=1 << 20, transcendentals=0),
        name="merge_parts",
    )(place, *parts)


def final_kernel(a_ref, b_ref, d_ref, e_ref, gate_ref, up_ref, gate_grad_ref, up_grad_ref):
    packed = decode(a_ref[...]) + decode(b_ref[...]) + decode(d_ref[...]) + decode(e_ref[...])
    tail = packed[192:208]
    tails = jnp.concatenate([tail] + [pltpu.roll(tail, LANES - 32 * k, 1) for k in range(1, 4)], axis=0)
    width = gate_ref.shape[1]
    for k in range(4):
        cols = slice(LANES * k, min(LANES * (k + 1), width))
        grad = packed[64 * k : 64 * k + 64] if k < 3 else tails[:, : width - 3 * LANES]
        gate = gate_ref[:, cols].astype(jnp.float32)
        up = up_ref[:, cols].astype(jnp.float32)
        s = jax.nn.sigmoid(gate)
        gate_grad_ref[:, cols] = (grad * up * s * (1.0 + gate * (1.0 - s))).astype(gate_grad_ref.dtype)
        up_grad_ref[:, cols] = (grad * (gate * s)).astype(up_grad_ref.dtype)


def final(parts, gate_pre, up_pre):
    return pl.pallas_call(
        final_kernel,
        out_shape=(jax.ShapeDtypeStruct(gate_pre.shape, gate_pre.dtype),) * 2,
        in_specs=[whole] * 6,
        out_specs=(whole, whole),
        compiler_params=pltpu.CompilerParams(vmem_limit_bytes=VMEM_BYTES),
        cost_estimate=pl.CostEstimate(flops=1, bytes_accessed=1, transcendentals=0),
        name="finish_grads",
    )(*parts, gate_pre, up_pre)


def weight_kernel(place_ref, hidden_ref, grad_ref, own_ref, their_ref):
    xl = place_ref[0]
    tokens = [hidden_ref[:, y1].reshape(512, hidden_ref.shape[3]) for y1 in range(2)]
    for out_ref, k in ((their_ref, 1 - xl), (own_ref, xl)):
        out_ref[...] = sum(
            lax.dot_general(
                tokens[y1],
                grad_ref[k, y1],
                (((0,), (0,)), ((), ())),
                preferred_element_type=jnp.float32,
            )
            for y1 in range(2)
        )


def weight_part(place, hidden, grad):
    return pl.pallas_call(
        weight_kernel,
        out_shape=(jax.ShapeDtypeStruct((hidden.shape[3], grad.shape[3]), jnp.float32),) * 2,
        in_specs=[scalars] + [whole] * 2,
        out_specs=(whole, whole),
        compiler_params=pltpu.CompilerParams(vmem_limit_bytes=VMEM_BYTES),
        cost_estimate=pl.CostEstimate(flops=2 * 2048 * 512 * 512, bytes_accessed=5 << 20, transcendentals=0),
        name="weight_part",
    )(place, hidden, grad)


def shift(array, axes, step):
    size = 2 ** len(axes)
    return lax.ppermute(array, axes, [(i, (i + step) % size) for i in range(size)])


def to_owner(array, step):
    pairs = [
        (a * 8 + far * 2 + b, b * 8 + (far + step) % 4 * 2 + a) for a in range(2) for far in range(4) for b in range(2)
    ]
    return lax.ppermute(array, ("xl",) + FAR + ("z0",), pairs)


def shards(gate_pre, up_pre, out_grad, down_weight):
    place = jnp.stack([lax.axis_index("xl"), lax.axis_index(Z[2:]), lax.axis_index(FAR)]).astype(jnp.int32)
    hid, feats = down_weight.shape
    gate_vals = gate_pre.astype(jnp.float32)
    hidden = (gate_vals * jax.nn.sigmoid(gate_vals) * up_pre.astype(jnp.float32)).astype(jnp.bfloat16)

    hidden = lax.ppermute(hidden, ("xl", "z0"), TURN)
    their_weight = lax.ppermute(down_weight, "xl", SWAP)
    copies = jnp.broadcast_to(out_grad.reshape(2, 1, 64, feats), (2, 16, 64, feats)).reshape(32, 64, feats)
    grad = lax.all_to_all(copies, ("xl",) + TENSOR, 0, 0)
    tokens = lax.all_gather(hidden, Z, axis=0, tiled=True)
    grad, tokens, their_weight = lax.optimization_barrier((grad, tokens, their_weight))
    blocks = grad.reshape(2, 2, 4, 2, 64, feats)

    halves = [k.astype(jnp.float16) for k in keep_part(True, place, blocks, down_weight, their_weight, tokens[:16])]
    near = [shift(h, Z, step) for h, step in zip(halves, (1, -1, 2, -2), strict=True)]
    (kept,) = keep_part(False, place, blocks, down_weight, their_weight, tokens[:16])
    own, theirs = weight_part(place, tokens.reshape(8, 2, 64, hid), grad.reshape(2, 2, 512, feats))
    near, kept, theirs = lax.optimization_barrier((near, kept, theirs))
    merged = merge(place, [kept] + [n.astype(jnp.float32) for n in near])
    got = lax.ppermute(theirs, "xl", SWAP)
    far = [to_owner(merged[k].astype(jnp.float16), k) for k in (2, 1, 3, 0)]
    weight_grad = (own + got) * 2048 ** (-0.5)
    far, weight_grad = lax.optimization_barrier((far, weight_grad))
    gate_grad, up_grad = final([f.astype(jnp.float32) for f in far], gate_pre, up_pre)
    return (gate_grad, up_grad, weight_grad)


def solution(mesh):
    bits = Mesh(np.asarray(mesh.devices).reshape((2,) * 9), DP + TENSOR)
    return jax.shard_map(
        shards,
        mesh=bits,
        in_specs=(P(DP, TENSOR), P(DP, TENSOR), P(TENSOR, DP), P(TENSOR, DP)),
        out_specs=(P(DP, TENSOR), P(DP, TENSOR), P(TENSOR, DP)),
        check_vma=False,
    )
```

```python
import functools

import jax
import jax.numpy as jnp
import numpy as np
from jax import lax
from jax.experimental import pallas as pl
from jax.experimental.pallas import tpu as pltpu
from jax.sharding import Mesh, PartitionSpec as P

Z = ("z3", "z2", "z1", "z0")
FAR = Z[:2]
DP = ("xl",) + Z
YX = ("y1", "y0", "xh")
TENSOR = YX + ("c",)
SWAP = [(0, 1), (1, 0)]
TURN = [(0, 0), (1, 2), (2, 1), (3, 3)]
LANES = 128
VMEM_BYTES = 16 * 1024 * 1024
whole = pl.BlockSpec(memory_space=pltpu.VMEM)
scalars = pl.BlockSpec(memory_space=pltpu.SMEM)


def pack(block):
    tail = block[:, 3 * LANES :]
    packed = tail[0:16]
    for k in range(1, 4):
        packed += pltpu.roll(tail[16 * k : 16 * k + 16], 32 * k, 1)
    return jnp.concatenate([block[:, LANES * k : LANES * (k + 1)] for k in range(3)] + [packed], axis=0)


def encode(packed):
    top = jnp.max(jnp.max(jnp.abs(packed), axis=0, keepdims=True), axis=1, keepdims=True)
    exponent = jnp.floor(jnp.log2(jnp.maximum(top, 1e-37)))
    scaled = packed * jnp.exp2(-exponent)
    return jnp.concatenate([scaled, jnp.broadcast_to(exponent, (16, LANES))], axis=0)


def decode(coded):
    return coded[:208] * jnp.exp2(coded[208:209])


def times(rows, weight):
    return lax.dot_general(rows, weight, (((1,), (1,)), ((), ())), preferred_element_type=jnp.float32)


def keep_kernel(for_others, place_ref, grad_ref, own_weight_ref, their_weight_ref, *refs):
    out_refs, padded = refs[1 if for_others else 0 : -1], refs[-1]
    hid, feats = own_weight_ref.shape
    xl, low = place_ref[0], place_ref[1]
    padded[:, hid:] = jnp.zeros_like(padded[:, hid:])
    padded[xl, :hid] = own_weight_ref[...]
    padded[1 - xl, :hid] = their_weight_ref[...]
    for ahead in (1, 3, 2) if for_others else (0,):
        place = lax.rem(low + ahead, 4)
        y1, core = lax.rem(place, 2), place // 2
        product = sum(times(grad_ref[k, y1, :, core].reshape(256, feats), padded[k]) for k in range(2))
        for far in range(4):
            vals = pack(product[64 * far : 64 * far + 64])
            if ahead == 0:
                out_refs[0][far] = vals
            elif ahead == 1:
                out_refs[0][far] = encode(vals)
            elif ahead == 3:
                out_refs[1][far] = encode(vals)
            else:
                out_refs[2 + far // 2][far % 2] = encode(vals)


def keep_part(for_others, place, grad, own_weight, their_weight, *tokens):
    shapes = [(4, 224, LANES), (4, 224, LANES), (2, 224, LANES), (2, 224, LANES)] if for_others else [(4, 208, LANES)]
    return pl.pallas_call(
        functools.partial(keep_kernel, for_others),
        out_shape=tuple(jax.ShapeDtypeStruct(s, jnp.float32) for s in shapes),
        in_specs=[scalars] + [whole] * (3 + len(tokens)),
        out_specs=(whole,) * len(shapes),
        scratch_shapes=[pltpu.VMEM((2, 512, own_weight.shape[1]), own_weight.dtype)],
        compiler_params=pltpu.CompilerParams(vmem_limit_bytes=VMEM_BYTES),
        cost_estimate=pl.CostEstimate(flops=2 * 256 * 1024 * 512, bytes_accessed=3 << 20, transcendentals=0),
        name="keep_others" if for_others else "keep_own",
    )(place, grad, own_weight, their_weight, *tokens)


def merge_kernel(place_ref, own_ref, up1_ref, down1_ref, up2_ref, down2_ref, *out_refs):
    for far in range(4):
        twice_ref = up2_ref if far < 2 else down2_ref
        vals = own_ref[far] + decode(up1_ref[far]) + decode(down1_ref[far]) + decode(twice_ref[far % 2])
        ahead = lax.rem(far - place_ref[2] + 4, 4)
        for k in range(4):

            @pl.when(ahead == k)
            def _(vals=vals, k=k):
                out_refs[k][...] = encode(vals)


def merge(place, parts):
    return pl.pallas_call(
        merge_kernel,
        out_shape=(jax.ShapeDtypeStruct((224, LANES), jnp.float32),) * 4,
        in_specs=[scalars] + [whole] * 5,
        out_specs=(whole,) * 4,
        compiler_params=pltpu.CompilerParams(vmem_limit_bytes=VMEM_BYTES),
        cost_estimate=pl.CostEstimate(flops=1 << 20, bytes_accessed=1 << 20, transcendentals=0),
        name="merge_parts",
    )(place, *parts)


def final_kernel(a_ref, b_ref, d_ref, e_ref, gate_ref, up_ref, gate_grad_ref, up_grad_ref):
    packed = decode(a_ref[...]) + decode(b_ref[...]) + decode(d_ref[...]) + decode(e_ref[...])
    tail = packed[192:208]
    tails = jnp.concatenate([tail] + [pltpu.roll(tail, LANES - 32 * k, 1) for k in range(1, 4)], axis=0)
    width = gate_ref.shape[1]
    for k in range(4):
        cols = slice(LANES * k, min(LANES * (k + 1), width))
        grad = packed[64 * k : 64 * k + 64] if k < 3 else tails[:, : width - 3 * LANES]
        gate = gate_ref[:, cols].astype(jnp.float32)
        up = up_ref[:, cols].astype(jnp.float32)
        s = jax.nn.sigmoid(gate)
        gate_grad_ref[:, cols] = (grad * up * s * (1.0 + gate * (1.0 - s))).astype(gate_grad_ref.dtype)
        up_grad_ref[:, cols] = (grad * (gate * s)).astype(up_grad_ref.dtype)


def final(parts, gate_pre, up_pre):
    return pl.pallas_call(
        final_kernel,
        out_shape=(jax.ShapeDtypeStruct(gate_pre.shape, gate_pre.dtype),) * 2,
        in_specs=[whole] * 6,
        out_specs=(whole, whole),
        compiler_params=pltpu.CompilerParams(vmem_limit_bytes=VMEM_BYTES),
        cost_estimate=pl.CostEstimate(flops=1, bytes_accessed=1, transcendentals=0),
        name="finish_grads",
    )(*parts, gate_pre, up_pre)


def weight_kernel(place_ref, hidden_ref, grad_ref, own_ref, their_ref):
    xl = place_ref[0]
    tokens = [hidden_ref[:, y1].reshape(512, hidden_ref.shape[3]) for y1 in range(2)]
    for out_ref, k in ((their_ref, 1 - xl), (own_ref, xl)):
        out_ref[...] = sum(
            lax.dot_general(
                tokens[y1],
                grad_ref[k, y1],
                (((0,), (0,)), ((), ())),
                preferred_element_type=jnp.float32,
            )
            for y1 in range(2)
        )


def weight_part(place, hidden, grad):
    return pl.pallas_call(
        weight_kernel,
        out_shape=(jax.ShapeDtypeStruct((hidden.shape[3], grad.shape[3]), jnp.float32),) * 2,
        in_specs=[scalars] + [whole] * 2,
        out_specs=(whole, whole),
        compiler_params=pltpu.CompilerParams(vmem_limit_bytes=VMEM_BYTES),
        cost_estimate=pl.CostEstimate(flops=2 * 2048 * 512 * 512, bytes_accessed=5 << 20, transcendentals=0),
        name="weight_part",
    )(place, hidden, grad)


def shift(array, axes, step):
    size = 2 ** len(axes)
    return lax.ppermute(array, axes, [(i, (i + step) % size) for i in range(size)])


def to_owner(array, step):
    pairs = [
        (a * 8 + far * 2 + b, b * 8 + (far + step) % 4 * 2 + a) for a in range(2) for far in range(4) for b in range(2)
    ]
    return lax.ppermute(array, ("xl",) + FAR + ("z0",), pairs)


def shards(gate_pre, up_pre, out_grad, down_weight):
    place = jnp.stack([lax.axis_index("xl"), lax.axis_index(Z[2:]), lax.axis_index(FAR)]).astype(jnp.int32)
    hid, feats = down_weight.shape
    gate_vals = gate_pre.astype(jnp.float32)
    hidden = (gate_vals * jax.nn.sigmoid(gate_vals) * up_pre.astype(jnp.float32)).astype(jnp.bfloat16)

    hidden = lax.ppermute(hidden, ("xl", "z0"), TURN)
    their_weight = lax.ppermute(down_weight, "xl", SWAP)
    copies = jnp.broadcast_to(out_grad.reshape(2, 1, 64, feats), (2, 16, 64, feats)).reshape(32, 64, feats)
    grad = lax.all_to_all(copies, ("xl",) + TENSOR, 0, 0)
    tokens = lax.all_gather(hidden, Z, axis=0, tiled=True)
    grad, tokens, their_weight = lax.optimization_barrier((grad, tokens, their_weight))
    blocks = grad.reshape(2, 2, 4, 2, 64, feats)

    halves = [k.astype(jnp.float16) for k in keep_part(True, place, blocks, down_weight, their_weight, tokens)]
    near = [shift(h, Z, step) for h, step in zip(halves, (1, -1, 2, -2), strict=True)]
    (kept,) = keep_part(False, place, blocks, down_weight, their_weight)
    own, theirs = weight_part(place, tokens.reshape(8, 2, 64, hid), grad.reshape(2, 2, 512, feats))
    near, kept, theirs = lax.optimization_barrier((near, kept, theirs))
    merged = merge(place, [kept] + [n.astype(jnp.float32) for n in near])
    got = lax.ppermute(theirs, "xl", SWAP)
    far = [to_owner(merged[k].astype(jnp.float16), k) for k in (2, 1, 3, 0)]
    weight_grad = (own + got) * 2048 ** (-0.5)
    far, weight_grad = lax.optimization_barrier((far, weight_grad))
    gate_grad, up_grad = final([f.astype(jnp.float32) for f in far], gate_pre, up_pre)
    return (gate_grad, up_grad, weight_grad)


def solution(mesh):
    bits = Mesh(np.asarray(mesh.devices).reshape((2,) * 9), DP + TENSOR)
    return jax.shard_map(
        shards,
        mesh=bits,
        in_specs=(P(DP, TENSOR), P(DP, TENSOR), P(TENSOR, DP), P(TENSOR, DP)),
        out_specs=(P(DP, TENSOR), P(DP, TENSOR), P(TENSOR, DP)),
        check_vma=False,
    )
```
